256 devices in a mesh: coord: 32 (over y, z), cohort: 8 (over x, core).
Axes of the slice: x: 4, y: 4, z: 8, core: 2. Of those that a mesh axis runs over, the one named last changes fastest.
Arguments:
- shapes: bfloat16 [8, 1024, 131072], P('cohort', None, 'coord'), may hold values from -6 to 6
- sketch_signs: int32 [8, 1024, 128], P('cohort'), may hold values from -1 to 1
- merge_sketch: float32 [2, 2, 128, 128], replicated, may hold values from -1.5 to 1.5
Outputs:
- basis: float32 [8, 131072, 128], P('cohort', 'coord')
- scores: float32 [8, 1024, 128], P('cohort', 'coord')
The draws below stay inside these ranges and needn't reach their ends.
All inputs are finite; a program needn't handle non-finite values.
Results may differ from the reference program's by a relative error of at most 0.0086.
Values sent between devices are 32-bit elements; how exact they have to be, the bound alone decides.
No kernel may reach another device: no remote copies, remote signals or barrier semaphores. Data moves between devices by JAX's collectives and lax.ppermute only.
A program may use at most 64 MiB of HBM per device.

```python
import math
import jax
import jax.numpy as jnp
from jax import lax

K = 128
SUBJ = 1024
LEVELS = 2
P_SIZE = 131072
COHORTS = 8


def draw_shapes(key, part):
    mode_key = jax.random.fold_in(key, 11)
    own_key = jax.random.fold_in(key, 12)
    coef_key = jax.random.fold_in(key, 13)
    noise_key = jax.random.fold_in(key, 14)
    modes = jax.random.normal(mode_key, (K, P_SIZE), jnp.float32)
    spread = 0.3 * jnp.power(0.97, jnp.arange(K, dtype=jnp.float32))
    coefs = jax.random.normal(coef_key, (COHORTS, SUBJ, K), jnp.float32) * spread
    own = jax.random.normal(own_key, (COHORTS, K, P_SIZE), jnp.float32)
    cohort_modes = modes[None] + 0.2 * own
    signal = jnp.einsum('csk,ckp->csp', coefs, cohort_modes)
    noise = 0.3 * jax.random.normal(noise_key, (COHORTS, SUBJ, P_SIZE), jnp.float32)
    values = signal + noise
    return jnp.clip(values, -6.0, 6.0).astype(jnp.bfloat16)


def draw_merge_sketch(key, part):
    mix_key = jax.random.fold_in(key, 21)
    noise = jnp.clip(jax.random.normal(mix_key, (LEVELS, 2, K, K), jnp.float32), -6.0, 6.0)
    noise = noise * (0.2 * K ** (-0.5))
    ident = jnp.eye(K, dtype=jnp.float32)
    lower_map = ident[None] + noise[:, 0]
    upper_map = noise[:, 1]
    return jnp.stack([lower_map, upper_map], axis=1)


def set_ends(entries, key, smallest, top_value):
    longest = entries.shape.index(max(entries.shape))
    spots = []
    for shift in (0, 1):
        where = [jax.random.randint(jax.random.fold_in(key, axis), (), 0, length) for axis, length in enumerate(entries.shape)]
        where[longest] = (where[longest] + shift) % entries.shape[longest]
        spots.append(tuple(where))
    return entries.at[spots[0]].set(smallest).at[spots[1]].set(top_value)


def setup_inputs(seed: int = 0) -> dict:
    splits = jax.random.split(jax.random.key(seed), 4)
    return {
        "shapes": draw_shapes(jax.random.fold_in(splits[3], 71), 0),
        "sketch_signs": set_ends(jax.random.randint(splits[1], (COHORTS, SUBJ, K), -1, 2), jax.random.fold_in(splits[1], 1), -1, 1).astype(jnp.int32),
        "merge_sketch": draw_merge_sketch(jax.random.fold_in(splits[3], 71), 0),
    }


def lower_inverse_t(gram):
    factor = jnp.linalg.cholesky(gram)
    ident = jnp.eye(gram.shape[0], dtype=gram.dtype)
    inverse = jax.scipy.linalg.solve_triangular(factor, ident, lower=True)
    return inverse.T

def orthonormal(mixed):
    gram = jnp.dot(mixed.T, mixed, precision=lax.Precision.HIGHEST)
    return jnp.dot(mixed, lower_inverse_t(gram), precision=lax.Precision.HIGHEST)

def reference(shapes, sketch_signs, merge_sketch):
    count = shapes.shape[0]
    centered_all = []
    bases = []
    for cohort in range(count):
        data = shapes[cohort].astype(jnp.float32)
        centered = (data - lax.optimization_barrier(jnp.mean(data, axis=0, keepdims=True))).astype(jnp.bfloat16)
        centered_all.append(centered)
        signs = sketch_signs[cohort].astype(jnp.bfloat16)
        sketch = jnp.dot(centered.T.astype(jnp.float32), signs.astype(jnp.float32), preferred_element_type=jnp.float32)
        bases.append(orthonormal(sketch))
    for level in range(LEVELS):
        merged = []
        for cohort in range(count):
            lower = cohort & ~(1 << level)
            upper = lower | 1 << level
            mixed = jnp.dot(bases[lower], merge_sketch[level, 0], precision=lax.Precision.HIGHEST)
            mixed = mixed + jnp.dot(bases[upper], merge_sketch[level, 1], precision=lax.Precision.HIGHEST)
            merged.append(orthonormal(mixed))
        bases = merged
    factor = 4.0 * math.sqrt(K / P_SIZE)
    basis_out = jnp.stack([b * math.sqrt(P_SIZE) for b in bases])
    score_out = jnp.stack([jnp.dot(centered_all[c].astype(jnp.float32), bases[c].astype(jnp.bfloat16).astype(jnp.float32), preferred_element_type=jnp.float32) * factor for c in range(count)])
    return (basis_out, score_out)
```

```python
import functools
import math

import jax
import jax.numpy as jnp
from jax import lax
from jax.experimental import pallas as pl
from jax.experimental.pallas import tpu as pltpu
from jax.sharding import PartitionSpec as P

HIGHEST = lax.Precision.HIGHEST
NN = (((1,), (0,)), ((), ()))
NT = (((1,), (1,)), ((), ()))
TN = (((0,), (0,)), ((), ()))
VMEM = pl.BlockSpec(memory_space=pltpu.VMEM)


def exact(a, b, dims):
    return lax.dot_general(a, b, dims, precision=HIGHEST, preferred_element_type=jnp.float32)


def cost(flops, bytes_accessed):
    return pl.CostEstimate(flops=flops, bytes_accessed=bytes_accessed, transcendentals=0)


def sketch_kernel(shapes_ref, signs_ref, centered_ref, sketch_ref, gram_ref):
    data = shapes_ref[...].astype(jnp.float32)
    mean = jnp.sum(data, axis=0, keepdims=True) * (1.0 / data.shape[0])
    centered = (data - mean).astype(jnp.bfloat16)
    centered_ref[...] = centered
    rows = lax.dot_general(signs_ref[...], centered, NN, preferred_element_type=jnp.float32)
    sketch_ref[...] = rows.T

    @pl.when(pl.program_id(0) == 0)
    def _():
        gram_ref[...] = jnp.zeros_like(gram_ref)

    gram_ref[...] += exact(rows, rows, NT)


def centered_sketch(shapes, signs):
    subjects, coords = shapes.shape
    modes = signs.shape[0]
    block = 512
    return pl.pallas_call(
        sketch_kernel,
        grid=(coords // block,),
        in_specs=[
            pl.BlockSpec((subjects, block), lambda i: (0, i)),
            pl.BlockSpec((modes, subjects), lambda i: (0, 0)),
        ],
        out_specs=[
            pl.BlockSpec((subjects, block), lambda i: (0, i)),
            pl.BlockSpec((block, modes), lambda i: (i, 0)),
            pl.BlockSpec((modes, modes), lambda i: (0, 0)),
        ],
        out_shape=[
            jax.ShapeDtypeStruct((subjects, coords), jnp.bfloat16),
            jax.ShapeDtypeStruct((coords, modes), jnp.float32),
            jax.ShapeDtypeStruct((modes, modes), jnp.float32),
        ],
        compiler_params=pltpu.CompilerParams(vmem_limit_bytes=40 << 20),
        cost_estimate=cost(8 << 30, 18 << 20),
        name="sketch",
    )(shapes, signs)


def wide(line):
    return jnp.broadcast_to(line, (8, 128))


def factor_inverse(matrix):
    count = matrix.shape[0] // 8
    tiles = [matrix[8 * i : 8 * i + 8, :] for i in range(count)]
    lane = lax.broadcasted_iota(jnp.int32, (8, 128), 1)
    sub = lax.broadcasted_iota(jnp.int32, (8, 128), 0)
    inverse = [(lane == sub + 8 * i).astype(jnp.float32) for i in range(count)]
    done = []
    for p in range(count):
        rows, ident_rows = tiles[p], inverse[p]
        cols = [wide(rows[:, 8 * p + t : 8 * p + t + 1]) for t in range(8)]
        d = [[wide(cols[t][s : s + 1, :]) if s >= t else None for t in range(8)] for s in range(8)]
        low = [[None] * 8 for _ in range(8)]
        inv = [[None] * 8 for _ in range(8)]
        for s in range(8):
            root = lax.rsqrt(d[s][s])
            for t in range(s + 1, 8):
                low[t][s] = d[t][s] * root
            for t in range(s + 1, 8):
                for u in range(s + 1, t + 1):
                    d[t][u] = d[t][u] - low[t][s] * low[u][s]
            inv[s][s] = root
            for c in range(s):
                acc = low[s][c] * inv[c][c]
                for u in range(c + 1, s):
                    acc = acc + low[s][u] * inv[u][c]
                inv[s][c] = -root * acc

        def solved(block):
            lines = [wide(block[s : s + 1, :]) for s in range(8)]
            return [sum(inv[t][s] * lines[s] for s in range(t + 1)) for t in range(8)]

        def solved_twice(lines):
            return [sum(inv[t][s] * lines[t] for t in range(7, s - 1, -1)) for s in range(8)]

        final = solved(ident_rows)
        tile = final[7]
        for t in range(7):
            tile = jnp.where(sub == t, final[t], tile)
        done.append(tile)
        if p == count - 1:
            break
        left, right = solved_twice(solved(rows)), solved_twice(final)
        for i in range(p + 1, count):
            c = [wide(tiles[i][:, 8 * p + s : 8 * p + s + 1]) for s in range(8)]
            tiles[i] = tiles[i] - sum(c[s] * left[s] for s in range(8))
            inverse[i] = inverse[i] - sum(c[s] * right[s] for s in range(8))
    return jnp.concatenate(done, axis=0)


def merged_gram(maps_lower, maps_upper, cross):
    return (
        exact(maps_lower, maps_lower, TN) + exact(maps_upper, maps_upper, TN) + cross + cross.T
    )


def first_levels_kernel(lower_ref, upper_ref, cross_ref, maps_ref, out_ref):
    lower = factor_inverse(lower_ref[...])
    upper = factor_inverse(upper_ref[...])
    lower = exact(lower, maps_ref[0], TN)
    upper = exact(upper, maps_ref[1], TN)
    cross = exact(lower, exact(cross_ref[...], upper, NN), TN)
    inverse = factor_inverse(merged_gram(maps_ref[0], maps_ref[1], cross))
    out_ref[0] = exact(lower, inverse, NT)
    out_ref[1] = exact(upper, inverse, NT)


def first_levels(lower, upper, cross, maps):
    return pl.pallas_call(
        first_levels_kernel,
        in_specs=[VMEM] * 4,
        out_specs=VMEM,
        out_shape=jax.ShapeDtypeStruct((2, *lower.shape), jnp.float32),
        cost_estimate=cost(18 << 30, 1 << 20),
        name="first_levels",
    )(lower, upper, cross, maps)


def last_level_kernel(cross_ref, maps_ref, self_ref, other_ref, near_ref, far_ref, out_ref):
    cross = exact(maps_ref[0], exact(cross_ref[...], maps_ref[1], NN), TN)
    inverse = factor_inverse(merged_gram(maps_ref[0], maps_ref[1], cross))
    out_ref[0:256, :] = exact(near_ref[...], exact(self_ref[...], inverse, NT), NN)
    out_ref[256:512, :] = exact(far_ref[...], exact(other_ref[...], inverse, NT), NN)


def last_level(cross, maps, own_map, other_map, near, far):
    return pl.pallas_call(
        last_level_kernel,
        in_specs=[VMEM] * 6,
        out_specs=VMEM,
        out_shape=jax.ShapeDtypeStruct((512, 128), jnp.float32),
        cost_estimate=cost(9 << 30, 1 << 20),
        name="last_level",
    )(cross, maps, own_map, other_map, near, far)


def output_kernel(scale, centered_ref, a_ref, b_ref, c_ref, d_ref, maps_ref, basis_ref, scores_ref):
    level = sum(
        exact(ref[...], maps_ref[128 * i : 128 * i + 128, :], NN)
        for i, ref in enumerate((a_ref, b_ref, c_ref, d_ref))
    )
    basis_ref[...] = level * scale

    @pl.when(pl.program_id(0) == 0)
    def _():
        scores_ref[...] = jnp.zeros_like(scores_ref)

    scores_ref[...] += jnp.dot(
        centered_ref[...], level.astype(jnp.bfloat16), preferred_element_type=jnp.float32
    )


def outputs(centered, sketches, maps, scale):
    subjects, coords = centered.shape
    block = 512
    rows = pl.BlockSpec((block, 128), lambda i: (i, 0))
    return pl.pallas_call(
        functools.partial(output_kernel, scale),
        grid=(coords // block,),
        in_specs=[
            pl.BlockSpec((subjects, block), lambda i: (0, i)),
            rows,
            rows,
            rows,
            rows,
            pl.BlockSpec((512, 128), lambda i: (0, 0)),
        ],
        out_specs=[rows, pl.BlockSpec((subjects, 128), lambda i: (0, 0))],
        out_shape=[
            jax.ShapeDtypeStruct((coords, 128), jnp.float32),
            jax.ShapeDtypeStruct((subjects, 128), jnp.float32),
        ],
        compiler_params=pltpu.CompilerParams(vmem_limit_bytes=40 << 20),
        cost_estimate=cost(8 << 30, 18 << 20),
        name="outputs",
    )(centered, *sketches, maps)


def sent_and_summed(lines, axis):
    count = lax.axis_size(axis)
    blocks = lax.all_to_all(lines.reshape(count, -1, lines.shape[-1]), axis, 0, 0, tiled=True)
    return jnp.sum(blocks, axis=0)


def summed(lines, axis):
    count = lax.axis_size(axis)
    part = sent_and_summed(lines, axis)
    blocks = lax.all_to_all(
        jnp.broadcast_to(part[None], (count, *part.shape)), axis, 0, 0, tiled=True
    )
    return blocks.reshape(lines.shape)


def across(shard, bit):
    return lax.ppermute(shard, "cohort", [(i, i ^ bit) for i in range(lax.axis_size("cohort"))])


def on_device(shapes, sketch_signs, merge_sketch):
    signs = sketch_signs[0].astype(jnp.bfloat16).T
    centered, own, gram = centered_sketch(shapes[0], signs)
    coords = own.shape[0]
    half = coords // 2
    position = lax.axis_index("cohort")
    upper_core = position & 1 == 1
    upper_chip = position >> 1 & 1
    kept, given = upper_chip * half, (1 - upper_chip) * half

    def half_of(array, start):
        return lax.dynamic_slice_in_dim(array, start, half, 0)

    far_kept = across(half_of(own, given), 2)
    mate = across(own, 1)
    far_given = across(half_of(own, kept), 2)

    core_rows = (position & 1) * half
    own_rows, mate_rows = half_of(own, core_rows), half_of(mate, core_rows)
    cross = exact(
        jnp.where(upper_core, mate_rows, own_rows),
        jnp.where(upper_core, own_rows, mate_rows),
        TN,
    )
    pair = summed(jnp.concatenate([gram, cross], axis=0), "coord")
    pair_mate = across(pair, 1)
    cross = pair[128:] + pair_mate[128:]
    lower_gram = jnp.where(upper_core, pair_mate[:128], pair[:128])
    upper_gram = jnp.where(upper_core, pair[:128], pair_mate[:128])
    near = first_levels(lower_gram, upper_gram, cross, merge_sketch[0])
    near = jnp.where(upper_core, near[::-1], near).reshape(256, 128)
    far = across(near, 2)

    far_cross = exact(
        jnp.concatenate([half_of(own, kept), half_of(mate, kept)], axis=1), far_kept, TN
    )
    far_cross = summed(far_cross, "coord")
    far_cross = exact(exact(near, far_cross, TN), far[:128], NN)
    far_cross = jnp.where(upper_chip == 1, far_cross.T, far_cross)
    far_cross = far_cross + across(far_cross, 1)
    far_cross = far_cross + across(far_cross, 2)

    own_map = lax.dynamic_index_in_dim(merge_sketch[1], upper_chip, 0, keepdims=False)
    other_map = lax.dynamic_index_in_dim(merge_sketch[1], 1 - upper_chip, 0, keepdims=False)
    maps = last_level(far_cross, merge_sketch[1], own_map, other_map, near, far)

    first = jnp.where(upper_chip == 1, far_given, far_kept)
    second = jnp.where(upper_chip == 1, far_kept, far_given)
    far_rows = jnp.concatenate([first, second], axis=0)
    far_mate = across(far_rows, 1)

    total = coords * lax.axis_size("coord")
    basis, scores = outputs(
        centered, (own, mate, far_rows, far_mate), maps, math.sqrt(total)
    )
    factor = 4.0 * math.sqrt(basis.shape[1] / total)
    return basis[None], (sent_and_summed(scores, "coord") * factor)[None]


def solution(mesh):
    placed = (P("cohort", None, "coord"), P("cohort", None, None), P())
    return jax.shard_map(
        on_device,
        mesh=mesh,
        in_specs=placed,
        out_specs=(P("cohort", "coord", None), P("cohort", "coord", None)),
        check_vma=False,
    )
```

```python
import functools
import math

import jax
import jax.numpy as jnp
from jax import lax
from jax.experimental import pallas as pl
from jax.experimental.pallas import tpu as pltpu
from jax.sharding import PartitionSpec as P

HIGHEST = lax.Precision.HIGHEST
NN = (((1,), (0,)), ((), ()))
NT = (((1,), (1,)), ((), ()))
TN = (((0,), (0,)), ((), ()))
VMEM = pl.BlockSpec(memory_space=pltpu.VMEM)
SMEM = pl.BlockSpec(memory_space=pltpu.SMEM)
BLOCK = 512
WIDE = 1024


def exact(a, b, dims):
    return lax.dot_general(a, b, dims, precision=HIGHEST, preferred_element_type=jnp.float32)


def product(a, b, dims):
    return lax.dot_general(a, b, dims, preferred_element_type=jnp.float32)


def halves(x):
    high = x.astype(jnp.bfloat16)
    return high, (x - high.astype(jnp.float32)).astype(jnp.bfloat16)


def vmem(mebibytes):
    return pltpu.CompilerParams(vmem_limit_bytes=mebibytes << 20)


def cost(flops, bytes_accessed):
    return pl.CostEstimate(flops=flops, bytes_accessed=bytes_accessed, transcendentals=0)


def struct(*shape):
    return jax.ShapeDtypeStruct(shape, jnp.float32)


def sketch_kernel(half_ref, shapes_ref, signs_ref, mean_ref, sketch_ref, turned_ref):
    @pl.when(pl.program_id(0) == 0)
    def _():
        turned_ref[...] = signs_ref[...].astype(jnp.float32).T.astype(jnp.bfloat16)

    data = shapes_ref[...].astype(jnp.float32)
    mean = jnp.sum(data, axis=0, keepdims=True) * (1.0 / data.shape[0])
    mean_ref[...] = mean
    centered = (data - mean).astype(jnp.bfloat16)
    sketch_ref[...] = product(turned_ref[...], centered, NN)


def sketched(half, shapes, signs):
    subjects, coords = shapes.shape
    steps = coords // 2 // BLOCK
    return pl.pallas_call(
        sketch_kernel,
        grid_spec=pltpu.PrefetchScalarGridSpec(
            num_scalar_prefetch=1,
            grid=(steps,),
            in_specs=[
                pl.BlockSpec((subjects, BLOCK), lambda i, half: (0, half[0] * steps + i)),
                pl.BlockSpec((subjects, 128), lambda i, half: (0, 0)),
            ],
            out_specs=[
                pl.BlockSpec((1, BLOCK), lambda i, half: (0, i)),
                pl.BlockSpec((128, BLOCK), lambda i, half: (0, i)),
            ],
            scratch_shapes=[pltpu.VMEM((128, subjects), jnp.bfloat16)],
        ),
        out_shape=[struct(1, coords // 2), struct(128, coords // 2)],
        cost_estimate=cost(1 << 30, 5 << 20),
        compiler_params=vmem(48),
        name="sketch",
    )(half, shapes, signs)


def cross_kernel(pairs, *refs):
    out_ref = refs[-1]
    total = None
    for p in range(pairs):
        first, second, other = refs[3 * p : 3 * p + 3]
        for start in range(0, first.shape[1], 1024):
            cut = pl.ds(start, 1024)
            high, low = halves(jnp.concatenate([first[:, cut], second[:, cut]], axis=0))
            other_high, other_low = halves(other[:, cut])
            both = product(high, jnp.concatenate([other_high, other_low], axis=0), NT)
            part = both[:, :128] + both[:, 128:] + product(low, other_high, NT)
            total = part if total is None else total + part
    out_ref[...] = total


def cross_grams(*groups):
    return pl.pallas_call(
        functools.partial(cross_kernel, len(groups)),
        in_specs=[VMEM] * (3 * len(groups)),
        out_specs=VMEM,
        out_shape=struct(256, 128),
        cost_estimate=cost(1 << 30, 4 << 20),
        compiler_params=vmem(12),
        name="cross_grams",
    )(*[array for group in groups for array in group])


def subject_kernel(started, half_ref, shapes_ref, mean_ref, first_ref, second_ref, *refs):
    out_ref = refs[-1]
    peers, lines, _ = out_ref.shape
    lines //= 2
    centered = (shapes_ref[...].astype(jnp.float32) - mean_ref[...]).astype(jnp.bfloat16)
    first, second = halves(first_ref[...]), halves(second_ref[...])
    sums = product(centered, jnp.concatenate([first[0], second[0]], axis=0), NT)
    sums = sums + product(centered, jnp.concatenate([first[1], second[1]], axis=0), NT)
    parts = [sums[:, 128 * k : 128 * k + 128].reshape(peers, lines, 128) for k in range(2)]

    @pl.when(pl.program_id(0) == 0)
    def _():
        for k, part in enumerate(parts):
            rows = slice(lines * k, lines * k + lines)
            out_ref[:, rows, :] = part + refs[0][:, rows, :] if started else part

    @pl.when(pl.program_id(0) > 0)
    def _():
        for k, part in enumerate(parts):
            out_ref[:, lines * k : lines * k + lines, :] += part


def subject_sums(peers, half, shapes, mean, first, second, start=None):
    subjects, coords = shapes.shape
    steps = coords // 2 // WIDE
    rows = pl.BlockSpec((128, WIDE), lambda i, half: (0, i))
    shape = (peers, 2 * subjects // peers, 128)
    whole = pl.BlockSpec(shape, lambda i, half: (0, 0, 0))
    given = [] if start is None else [start]
    return pl.pallas_call(
        functools.partial(subject_kernel, bool(given)),
        grid_spec=pltpu.PrefetchScalarGridSpec(
            num_scalar_prefetch=1,
            grid=(steps,),
            in_specs=[
                pl.BlockSpec((subjects, WIDE), lambda i, half: (0, half[0] * steps + i)),
                pl.BlockSpec((1, WIDE), lambda i, half: (0, i)),
                rows,
                rows,
            ]
            + [whole] * len(given),
            out_specs=whole,
        ),
        out_shape=struct(*shape),
        cost_estimate=cost(4 << 30, 6 << 20),
        compiler_params=vmem(44),
        name="subject_sums",
    )(half, shapes, mean, first, second, *given)


def wide(line):
    return jnp.broadcast_to(line, (8, 128))


def factor_inverse(matrix):
    count = matrix.shape[0] // 8
    tiles = [matrix[8 * i : 8 * i + 8, :] for i in range(count)]
    lane = lax.broadcasted_iota(jnp.int32, (8, 128), 1)
    sub = lax.broadcasted_iota(jnp.int32, (8, 128), 0)
    inverse = [(lane == sub + 8 * i).astype(jnp.float32) for i in range(count)]
    done = []
    for p in range(count):
        rows, ident_rows = tiles[p], inverse[p]
        cols = [wide(rows[:, 8 * p + t : 8 * p + t + 1]) for t in range(8)]
        d = [[wide(cols[t][s : s + 1, :]) if s >= t else None for t in range(8)] for s in range(8)]
        low = [[None] * 8 for _ in range(8)]
        inv = [[None] * 8 for _ in range(8)]
        for s in range(8):
            root = lax.rsqrt(d[s][s])
            for t in range(s + 1, 8):
                low[t][s] = d[t][s] * root
            for t in range(s + 1, 8):
                for u in range(s + 1, t + 1):
                    d[t][u] = d[t][u] - low[t][s] * low[u][s]
            inv[s][s] = root
            for c in range(s):
                acc = low[s][c] * inv[c][c]
                for u in range(c + 1, s):
                    acc = acc + low[s][u] * inv[u][c]
                inv[s][c] = -root * acc

        def solved(block):
            lines = [wide(block[s : s + 1, :]) for s in range(8)]
            return [sum(inv[t][s] * lines[s] for s in range(t + 1)) for t in range(8)]

        def solved_twice(lines):
            return [sum(inv[t][s] * lines[t] for t in range(7, s - 1, -1)) for s in range(8)]

        final = solved(ident_rows)
        tile = final[7]
        for t in range(7):
            tile = jnp.where(sub == t, final[t], tile)
        done.append(tile)
        if p == count - 1:
            break
        left, right = solved_twice(solved(rows)), solved_twice(final)
        for i in range(p + 1, count):
            c = [wide(tiles[i][:, 8 * p + s : 8 * p + s + 1]) for s in range(8)]
            tiles[i] = tiles[i] - sum(c[s] * left[s] for s in range(8))
            inverse[i] = inverse[i] - sum(c[s] * right[s] for s in range(8))
    return jnp.concatenate(done, axis=0)


def merged_gram(maps_ref, cross):
    lower, upper = maps_ref[0, 0], maps_ref[0, 1]
    return exact(lower, lower, TN) + exact(upper, upper, TN) + cross + cross.T


def part_of(shape, *index):
    return pl.BlockSpec(shape, lambda i: index)


def level_maps(level):
    return part_of((1, 2, 128, 128), level, 0, 0, 0)


def own_level_kernel(side_ref, gram_ref, maps_ref, out_ref):
    inverse = factor_inverse(gram_ref[...].reshape(128, 128))
    out_ref[...] = exact(inverse, maps_ref[0, side_ref[0]], TN)


def own_level(side, pair, maps):
    return pl.pallas_call(
        own_level_kernel,
        grid=(1,),
        in_specs=[SMEM, part_of((16, 8, 128), 0, 0, 0), level_maps(0)],
        out_specs=VMEM,
        out_shape=struct(128, 128),
        cost_estimate=cost(7 << 30, 1 << 20),
        compiler_params=vmem(4),
        name="own_level",
    )(side, pair, maps)


def pair_level_kernel(own_ref, mate_ref, cross_ref, maps_ref, out_ref):
    own, mate = own_ref[...], mate_ref[...]
    cross = exact(mate, exact(cross_ref[...].reshape(128, 128), own, NN), TN)
    inverse = factor_inverse(merged_gram(maps_ref, cross))
    out_ref[0:128, :] = exact(own, inverse, NT)
    out_ref[128:256, :] = exact(mate, inverse, NT)


def pair_level(own, mate, pair, maps):
    return pl.pallas_call(
        pair_level_kernel,
        grid=(1,),
        in_specs=[VMEM, VMEM, part_of((16, 8, 128), 1, 0, 0), level_maps(0)],
        out_specs=VMEM,
        out_shape=struct(256, 128),
        cost_estimate=cost(8 << 30, 1 << 20),
        compiler_params=vmem(4),
        name="pair_level",
    )(own, mate, pair, maps)


def far_cross_kernel(side_ref, near_ref, cross_ref, far_ref, out_ref):
    cross = exact(near_ref[...], cross_ref[...].reshape(256, 128), TN)
    cross = exact(cross, far_ref[0:128, :], NN)
    out_ref[...] = jnp.where(side_ref[0] == 1, cross.T, cross)


def far_cross_term(side, near, cross, far):
    return pl.pallas_call(
        far_cross_kernel,
        grid=(1,),
        in_specs=[SMEM, VMEM, part_of((32, 8, 128), 0, 0, 0), VMEM],
        out_specs=VMEM,
        out_shape=struct(128, 128),
        cost_estimate=cost(1 << 29, 1 << 20),
        compiler_params=vmem(4),
        name="far_cross",
    )(side, near, cross, far)


def mixed(a, b, dims):
    (a_high, a_low), (b_high, b_low) = halves(a), halves(b)
    return product(a_high, b_high, dims) + (
        product(a_high, b_low, dims) + product(a_low, b_high, dims)
    )


def far_terms_kernel(sums_ref, far_ref, out_ref):
    peers, lines, _ = out_ref.shape
    total = None
    for k in range(2):
        sums = sums_ref[:, lines * k : lines * k + lines, :].reshape(peers * lines, 128)
        part = mixed(sums, far_ref[128 * k : 128 * k + 128, :], NN)
        total = part if total is None else total + part
    out_ref[...] = total.reshape(out_ref.shape)


def far_terms(sums, far):
    peers, lines, width = sums.shape
    return pl.pallas_call(
        far_terms_kernel,
        in_specs=[VMEM] * 2,
        out_specs=VMEM,
        out_shape=struct(peers, lines // 2, width),
        cost_estimate=cost(1 << 29, 2 << 20),
        compiler_params=vmem(10),
        name="far_terms",
    )(sums, far)


def last_level_kernel(scale, side_ref, cross_ref, maps_ref, near_ref, far_ref, *refs):
    sources, (basis_ref, own_ref, other_ref, held, done, sems, out_sems) = refs[:8], refs[8:]
    side = side_ref[0]
    half = held.shape[2]
    loads = [
        pltpu.make_async_copy(
            source, held.at[k // 4, pl.ds(k % 4 * 128, 128), :], sems.at[k]
        )
        for k, source in enumerate(sources)
    ]
    for load in loads:
        load.start()
    lower, upper = maps_ref[0, 0], maps_ref[0, 1]
    cross = exact(exact(lower, cross_ref[...], TN), upper, NN)
    inverse = factor_inverse(merged_gram(maps_ref, cross))
    own = exact(maps_ref[0, side], inverse, NT)
    other = exact(maps_ref[0, 1 - side], inverse, NT)
    near = exact(near_ref[...], own, NN)
    own_ref[...] = near
    other_ref[...] = other
    maps = jnp.concatenate([near, exact(far_ref[...], other, NN)], axis=0).T * scale
    maps_high, maps_low = halves(maps)
    both_maps = jnp.concatenate([maps_high, maps_low], axis=0)
    stores = []
    for slot, start in ((0, side * half), (1, (1 - side) * half)):
        for load in loads[4 * slot : 4 * slot + 4]:
            load.wait()
        for chunk in range(half // BLOCK):
            high, low = halves(held[slot, :, chunk * BLOCK : chunk * BLOCK + BLOCK])
            both = product(both_maps, high, NN)
            rows = (both[:128] + both[128:] + product(maps_high, low, NN)).T
            k = slot * (half // BLOCK) + chunk
            done[k] = rows
            store = pltpu.make_async_copy(
                done.at[k], basis_ref.at[pl.ds(start + chunk * BLOCK, BLOCK), :], out_sems.at[k]
            )
            store.start()
            stores.append(store)
    for store in stores:
        store.wait()


def last_level(side, cross, maps, near, far, kept, given, scale):
    half = kept[0].shape[1]
    chunks = 2 * half // BLOCK
    return pl.pallas_call(
        functools.partial(last_level_kernel, scale),
        grid=(1,),
        in_specs=[SMEM, VMEM, level_maps(1), VMEM, VMEM]
        + [pl.BlockSpec(memory_space=pl.ANY)] * 8,
        out_specs=[pl.BlockSpec(memory_space=pl.ANY), VMEM, VMEM],
        out_shape=[struct(2 * half, 128), struct(256, 128), struct(128, 128)],
        scratch_shapes=[
            pltpu.VMEM((2, 512, half), jnp.float32),
            pltpu.VMEM((chunks, BLOCK, 128), jnp.float32),
            pltpu.SemaphoreType.DMA((8,)),
            pltpu.SemaphoreType.DMA((chunks,)),
        ],
        cost_estimate=cost(12 << 30, 10 << 20),
        compiler_params=vmem(50),
        name="last_level",
    )(side, cross, maps, near, far, *kept, *given)


def scores_kernel(scale, near_ref, far_ref, own_ref, other_ref, out_ref):
    lines = out_ref.shape[0]
    total = mixed(jnp.sum(far_ref[...], axis=0), other_ref[...], NN)
    for k in range(2):
        rows = near_ref[lines * k : lines * k + lines, :]
        total = total + mixed(rows, own_ref[128 * k : 128 * k + 128, :], NN)
    out_ref[...] = total * scale


def scores_of(near, far, own, other, scale):
    return pl.pallas_call(
        functools.partial(scores_kernel, scale),
        in_specs=[VMEM] * 4,
        out_specs=VMEM,
        out_shape=struct(near.shape[0] // 2, 128),
        cost_estimate=cost(1 << 29, 1 << 20),
        compiler_params=vmem(4),
        name="scores",
    )(near, far, own, other)


def to_each(lines, axis):
    count = lax.axis_size(axis)
    return lines.reshape(count, -1, lines.shape[-1])


def to_all(part, axis):
    return jnp.broadcast_to(part[None], (lax.axis_size(axis), *part.shape))


def exchanged(blocks, axis):
    return lax.all_to_all(blocks, axis, 0, 0, tiled=True)


def across(shard, bit):
    return lax.ppermute(shard, "cohort", [(i, i ^ bit) for i in range(lax.axis_size("cohort"))])


def after(value, *others):
    return lax.optimization_barrier((value, *others))[0]


def on_device(shapes, sketch_signs, merge_sketch):
    shapes, signs = shapes[0], sketch_signs[0]
    peers = lax.axis_size("coord")
    position = lax.axis_index("cohort")
    side = (position & 1).reshape(1)
    upper = (position >> 1 & 1).reshape(1)

    mean_given, own_given = sketched(1 - upper, shapes, signs)
    far_kept = across(own_given, 2)
    mean_kept, own_kept = sketched(upper, shapes, signs)
    mate_given = across(own_given, 1)
    mate_kept = across(own_kept, 1)
    pair = cross_grams((own_given, mate_given, own_given), (own_kept, mate_kept, own_kept))
    later = after(shapes, pair)
    pair = exchanged(to_each(pair, "coord"), "coord")
    near_sums = subject_sums(peers, 1 - upper, later, mean_given, own_given, mate_given)
    near_sums = subject_sums(peers, upper, later, mean_kept, own_kept, mate_kept, near_sums)
    pair_part = jnp.sum(pair, axis=0)
    lines = pair_part.shape[0]
    far_kept = after(far_kept, near_sums, pair_part)

    far_cross = cross_grams((own_kept, mate_kept, far_kept))
    far_given = across(after(own_kept, far_kept), 2)
    far_mate_kept = across(far_kept, 1)
    both = exchanged(
        jnp.concatenate([to_all(pair_part, "coord"), to_each(far_cross, "coord")], axis=1), "coord"
    )
    far_sums = subject_sums(peers, upper, shapes, mean_kept, far_kept, far_mate_kept)
    both = after(both, far_sums)
    far_part = jnp.sum(both[:, lines:], axis=0)
    far_cross = exchanged(
        jnp.concatenate([to_all(far_part, "coord"), near_sums], axis=1), "coord"
    )

    own_map = own_level(side, both, merge_sketch)
    mate_map = across(own_map, 1)
    near = pair_level(own_map, mate_map, both, merge_sketch)
    far = across(near, 2)
    far_given = after(far_given, own_map)
    far_mate_given = across(far_given, 1)
    far_sums = subject_sums(
        peers, 1 - upper, after(shapes, near), mean_given, far_given, far_mate_given, far_sums
    )

    far = after(far, far_sums)
    near_sums = jnp.sum(far_cross[:, lines:], axis=0)
    far_cross = far_cross_term(upper, near, far_cross, far)
    far_cross = far_cross + across(far_cross, 1)
    far_sums = exchanged(far_terms(far_sums, after(far, far_cross)), "coord")
    far_cross = far_cross + across(far_cross, 2)

    total = shapes.shape[1] * peers
    basis, own_map, other_map = last_level(
        upper,
        far_cross,
        merge_sketch,
        near,
        far,
        (own_kept, mate_kept, far_kept, far_mate_kept),
        (own_given, mate_given, far_given, far_mate_given),
        math.sqrt(total),
    )
    factor = 4.0 * math.sqrt(basis.shape[1] / total)
    scores = scores_of(near_sums, far_sums, own_map, other_map, factor)
    return basis[None], scores[None]


def solution(mesh):
    placed = (P("cohort", None, "coord"), P("cohort", None, None), P())
    return jax.shard_map(
        on_device,
        mesh=mesh,
        in_specs=placed,
        out_specs=(P("cohort", "coord", None), P("cohort", "coord", None)),
        check_vma=False,
    )
```

```python
import functools
import math

import jax
import jax.numpy as jnp
from jax import lax
from jax.experimental import pallas as pl
from jax.experimental.pallas import tpu as pltpu
from jax.sharding import PartitionSpec as P

HIGHEST = lax.Precision.HIGHEST
NN = (((1,), (0,)), ((), ()))
NT = (((1,), (1,)), ((), ()))
TN = (((0,), (0,)), ((), ()))
VMEM = pl.BlockSpec(memory_space=pltpu.VMEM)
SMEM = pl.BlockSpec(memory_space=pltpu.SMEM)
BLOCK = 512
WIDE = 1024


def exact(a, b, dims):
    return lax.dot_general(a, b, dims, precision=HIGHEST, preferred_element_type=jnp.float32)


def product(a, b, dims):
    return lax.dot_general(a, b, dims, preferred_element_type=jnp.float32)


def halves(x):
    high = x.astype(jnp.bfloat16)
    return high, (x - high.astype(jnp.float32)).astype(jnp.bfloat16)


def vmem(mebibytes):
    return pltpu.CompilerParams(vmem_limit_bytes=mebibytes << 20)


def cost(flops, bytes_accessed):
    return pl.CostEstimate(flops=flops, bytes_accessed=bytes_accessed, transcendentals=0)


def struct(*shape):
    return jax.ShapeDtypeStruct(shape, jnp.float32)


def sketch_kernel(half_ref, shapes_ref, signs_ref, mean_ref, sketch_ref, turned_ref):
    @pl.when(pl.program_id(0) == 0)
    def _():
        turned_ref[...] = signs_ref[...].astype(jnp.float32).T.astype(jnp.bfloat16)

    data = shapes_ref[...].astype(jnp.float32)
    mean = jnp.sum(data, axis=0, keepdims=True) * (1.0 / data.shape[0])
    mean_ref[...] = mean
    centered = (data - mean).astype(jnp.bfloat16)
    sketch_ref[...] = product(turned_ref[...], centered, NN)


def sketched(half, shapes, signs):
    subjects, coords = shapes.shape
    steps = coords // 2 // BLOCK
    return pl.pallas_call(
        sketch_kernel,
        grid_spec=pltpu.PrefetchScalarGridSpec(
            num_scalar_prefetch=1,
            grid=(steps,),
            in_specs=[
                pl.BlockSpec((subjects, BLOCK), lambda i, half: (0, half[0] * steps + i)),
                pl.BlockSpec((subjects, 128), lambda i, half: (0, 0)),
            ],
            out_specs=[
                pl.BlockSpec((1, BLOCK), lambda i, half: (0, i)),
                pl.BlockSpec((128, BLOCK), lambda i, half: (0, i)),
            ],
            scratch_shapes=[pltpu.VMEM((128, subjects), jnp.bfloat16)],
        ),
        out_shape=[struct(1, coords // 2), struct(128, coords // 2)],
        cost_estimate=cost(1 << 30, 5 << 20),
        compiler_params=vmem(48),
        name="sketch",
    )(half, shapes, signs)


def cross_kernel(pairs, *refs):
    out_ref = refs[-1]
    total = None
    for p in range(pairs):
        first, second, other = refs[3 * p : 3 * p + 3]
        for start in range(0, first.shape[1], 1024):
            cut = pl.ds(start, 1024)
            high, low = halves(jnp.concatenate([first[:, cut], second[:, cut]], axis=0))
            other_high, other_low = halves(other[:, cut])
            both = product(high, jnp.concatenate([other_high, other_low], axis=0), NT)
            part = both[:, :128] + both[:, 128:] + product(low, other_high, NT)
            total = part if total is None else total + part
    out_ref[...] = total


def cross_grams(*groups):
    return pl.pallas_call(
        functools.partial(cross_kernel, len(groups)),
        in_specs=[VMEM] * (3 * len(groups)),
        out_specs=VMEM,
        out_shape=struct(256, 128),
        cost_estimate=cost(1 << 30, 4 << 20),
        compiler_params=vmem(12),
        name="cross_grams",
    )(*[array for group in groups for array in group])


def subject_kernel(started, half_ref, shapes_ref, mean_ref, first_ref, second_ref, *refs):
    out_ref = refs[-1]
    peers, lines, _ = out_ref.shape
    lines //= 2
    centered = (shapes_ref[...].astype(jnp.float32) - mean_ref[...]).astype(jnp.bfloat16)
    first, second = halves(first_ref[...]), halves(second_ref[...])
    sums = product(centered, jnp.concatenate([first[0], second[0]], axis=0), NT)
    sums = sums + product(centered, jnp.concatenate([first[1], second[1]], axis=0), NT)
    parts = [sums[:, 128 * k : 128 * k + 128].reshape(peers, lines, 128) for k in range(2)]

    @pl.when(pl.program_id(0) == 0)
    def _():
        for k, part in enumerate(parts):
            rows = slice(lines * k, lines * k + lines)
            out_ref[:, rows, :] = part + refs[0][:, rows, :] if started else part

    @pl.when(pl.program_id(0) > 0)
    def _():
        for k, part in enumerate(parts):
            out_ref[:, lines * k : lines * k + lines, :] += part


def subject_sums(peers, half, shapes, mean, first, second, start=None):
    subjects, coords = shapes.shape
    steps = coords // 2 // WIDE
    rows = pl.BlockSpec((128, WIDE), lambda i, half: (0, i))
    shape = (peers, 2 * subjects // peers, 128)
    whole = pl.BlockSpec(shape, lambda i, half: (0, 0, 0))
    given = [] if start is None else [start]
    return pl.pallas_call(
        functools.partial(subject_kernel, bool(given)),
        grid_spec=pltpu.PrefetchScalarGridSpec(
            num_scalar_prefetch=1,
            grid=(steps,),
            in_specs=[
                pl.BlockSpec((subjects, WIDE), lambda i, half: (0, half[0] * steps + i)),
                pl.BlockSpec((1, WIDE), lambda i, half: (0, i)),
                rows,
                rows,
            ]
            + [whole] * len(given),
            out_specs=whole,
        ),
        out_shape=struct(*shape),
        cost_estimate=cost(4 << 30, 6 << 20),
        compiler_params=vmem(44),
        name="subject_sums",
    )(half, shapes, mean, first, second, *given)


def wide(line):
    return jnp.broadcast_to(line, (8, 128))


def factor_inverse(matrix):
    count = matrix.shape[0] // 8
    tiles = [matrix[8 * i : 8 * i + 8, :] for i in range(count)]
    lane = lax.broadcasted_iota(jnp.int32, (8, 128), 1)
    sub = lax.broadcasted_iota(jnp.int32, (8, 128), 0)
    inverse = [(lane == sub + 8 * i).astype(jnp.float32) for i in range(count)]
    done = []
    for p in range(count):
        rows, ident_rows = tiles[p], inverse[p]
        cols = [wide(rows[:, 8 * p + t : 8 * p + t + 1]) for t in range(8)]
        d = [[wide(cols[t][s : s + 1, :]) if s >= t else None for t in range(8)] for s in range(8)]
        low = [[None] * 8 for _ in range(8)]
        inv = [[None] * 8 for _ in range(8)]
        for s in range(8):
            root = lax.rsqrt(d[s][s])
            for t in range(s + 1, 8):
                low[t][s] = d[t][s] * root
            for t in range(s + 1, 8):
                for u in range(s + 1, t + 1):
                    d[t][u] = d[t][u] - low[t][s] * low[u][s]
            inv[s][s] = root
            for c in range(s):
                acc = low[s][c] * inv[c][c]
                for u in range(c + 1, s):
                    acc = acc + low[s][u] * inv[u][c]
                inv[s][c] = -root * acc

        def solved(block):
            lines = [wide(block[s : s + 1, :]) for s in range(8)]
            return [sum(inv[t][s] * lines[s] for s in range(t + 1)) for t in range(8)]

        def solved_twice(lines):
            return [sum(inv[t][s] * lines[t] for t in range(7, s - 1, -1)) for s in range(8)]

        final = solved(ident_rows)
        tile = final[7]
        for t in range(7):
            tile = jnp.where(sub == t, final[t], tile)
        done.append(tile)
        if p == count - 1:
            break
        left, right = solved_twice(solved(rows)), solved_twice(final)
        for i in range(p + 1, count):
            c = [wide(tiles[i][:, 8 * p + s : 8 * p + s + 1]) for s in range(8)]
            tiles[i] = tiles[i] - sum(c[s] * left[s] for s in range(8))
            inverse[i] = inverse[i] - sum(c[s] * right[s] for s in range(8))
    return jnp.concatenate(done, axis=0)


def merged_gram(maps_ref, cross):
    lower, upper = maps_ref[0, 0], maps_ref[0, 1]
    return exact(lower, lower, TN) + exact(upper, upper, TN) + cross + cross.T


def part_of(shape, *index):
    return pl.BlockSpec(shape, lambda i: index)


def level_maps(level):
    return part_of((1, 2, 128, 128), level, 0, 0, 0)


def own_level_kernel(side_ref, gram_ref, maps_ref, out_ref):
    inverse = factor_inverse(gram_ref[...].reshape(128, 128))
    out_ref[...] = exact(inverse, maps_ref[0, side_ref[0]], TN)


def own_level(side, pair, maps):
    return pl.pallas_call(
        own_level_kernel,
        grid=(1,),
        in_specs=[SMEM, part_of((16, 8, 128), 0, 0, 0), level_maps(0)],
        out_specs=VMEM,
        out_shape=struct(128, 128),
        cost_estimate=cost(7 << 30, 1 << 20),
        compiler_params=vmem(4),
        name="own_level",
    )(side, pair, maps)


def pair_level_kernel(own_ref, mate_ref, cross_ref, maps_ref, out_ref):
    own, mate = own_ref[...], mate_ref[...]
    cross = exact(mate, exact(cross_ref[...].reshape(128, 128), own, NN), TN)
    inverse = factor_inverse(merged_gram(maps_ref, cross))
    out_ref[0:128, :] = exact(own, inverse, NT)
    out_ref[128:256, :] = exact(mate, inverse, NT)


def pair_level(own, mate, pair, maps):
    return pl.pallas_call(
        pair_level_kernel,
        grid=(1,),
        in_specs=[VMEM, VMEM, part_of((16, 8, 128), 1, 0, 0), level_maps(0)],
        out_specs=VMEM,
        out_shape=struct(256, 128),
        cost_estimate=cost(8 << 30, 1 << 20),
        compiler_params=vmem(4),
        name="pair_level",
    )(own, mate, pair, maps)


def far_cross_kernel(side_ref, near_ref, cross_ref, far_ref, out_ref):
    cross = exact(near_ref[...], cross_ref[...].reshape(256, 128), TN)
    cross = exact(cross, far_ref[0:128, :], NN)
    out_ref[...] = jnp.where(side_ref[0] == 1, cross.T, cross)


def far_cross_term(side, near, cross, far):
    return pl.pallas_call(
        far_cross_kernel,
        grid=(1,),
        in_specs=[SMEM, VMEM, part_of((32, 8, 128), 0, 0, 0), VMEM],
        out_specs=VMEM,
        out_shape=struct(128, 128),
        cost_estimate=cost(1 << 29, 1 << 20),
        compiler_params=vmem(4),
        name="far_cross",
    )(side, near, cross, far)


def mixed(a, b, dims):
    (a_high, a_low), (b_high, b_low) = halves(a), halves(b)
    return product(a_high, b_high, dims) + (
        product(a_high, b_low, dims) + product(a_low, b_high, dims)
    )


def far_terms_kernel(kept_ref, given_ref, far_ref, out_ref):
    peers, lines, _ = out_ref.shape
    total = None
    for k in range(2):
        rows = slice(lines * k, lines * k + lines)
        sums = (kept_ref[:, rows, :] + given_ref[:, rows, :]).reshape(peers * lines, 128)
        part = mixed(sums, far_ref[128 * k : 128 * k + 128, :], NN)
        total = part if total is None else total + part
    out_ref[...] = total.reshape(out_ref.shape)


def far_terms(kept, given, far):
    peers, lines, width = kept.shape
    return pl.pallas_call(
        far_terms_kernel,
        in_specs=[VMEM] * 3,
        out_specs=VMEM,
        out_shape=struct(peers, lines // 2, width),
        cost_estimate=cost(1 << 29, 2 << 20),
        compiler_params=vmem(10),
        name="far_terms",
    )(kept, given, far)


def last_level_kernel(scale, side_ref, cross_ref, maps_ref, near_ref, far_ref, *refs):
    sources, (basis_ref, own_ref, other_ref, held, done, sems, out_sems) = refs[:8], refs[8:]
    side = side_ref[0]
    half = held.shape[2]
    loads = [
        pltpu.make_async_copy(
            source, held.at[k // 4, pl.ds(k % 4 * 128, 128), :], sems.at[k]
        )
        for k, source in enumerate(sources)
    ]
    for load in loads:
        load.start()
    lower, upper = maps_ref[0, 0], maps_ref[0, 1]
    cross = exact(exact(lower, cross_ref[...], TN), upper, NN)
    inverse = factor_inverse(merged_gram(maps_ref, cross))
    own = exact(maps_ref[0, side], inverse, NT)
    other = exact(maps_ref[0, 1 - side], inverse, NT)
    near = exact(near_ref[...], own, NN)
    own_ref[...] = near
    other_ref[...] = other
    maps = jnp.concatenate([near, exact(far_ref[...], other, NN)], axis=0).T * scale
    maps_high, maps_low = halves(maps)
    both_maps = jnp.concatenate([maps_high, maps_low], axis=0)
    stores = []
    for slot, start in ((0, side * half), (1, (1 - side) * half)):
        for load in loads[4 * slot : 4 * slot + 4]:
            load.wait()
        for chunk in range(half // BLOCK):
            high, low = halves(held[slot, :, chunk * BLOCK : chunk * BLOCK + BLOCK])
            both = product(both_maps, high, NN)
            rows = (both[:128] + both[128:] + product(maps_high, low, NN)).T
            k = slot * (half // BLOCK) + chunk
            done[k] = rows
            store = pltpu.make_async_copy(
                done.at[k], basis_ref.at[pl.ds(start + chunk * BLOCK, BLOCK), :], out_sems.at[k]
            )
            store.start()
            stores.append(store)
    for store in stores:
        store.wait()


def last_level(side, cross, maps, near, far, kept, given, scale):
    half = kept[0].shape[1]
    chunks = 2 * half // BLOCK
    return pl.pallas_call(
        functools.partial(last_level_kernel, scale),
        grid=(1,),
        in_specs=[SMEM, VMEM, level_maps(1), VMEM, VMEM]
        + [pl.BlockSpec(memory_space=pl.ANY)] * 8,
        out_specs=[pl.BlockSpec(memory_space=pl.ANY), VMEM, VMEM],
        out_shape=[struct(2 * half, 128), struct(256, 128), struct(128, 128)],
        scratch_shapes=[
            pltpu.VMEM((2, 512, half), jnp.float32),
            pltpu.VMEM((chunks, BLOCK, 128), jnp.float32),
            pltpu.SemaphoreType.DMA((8,)),
            pltpu.SemaphoreType.DMA((chunks,)),
        ],
        cost_estimate=cost(12 << 30, 10 << 20),
        compiler_params=vmem(50),
        name="last_level",
    )(side, cross, maps, near, far, *kept, *given)


def scores_kernel(scale, near_ref, far_ref, own_ref, other_ref, out_ref):
    lines = out_ref.shape[0]
    total = mixed(jnp.sum(far_ref[...], axis=0), other_ref[...], NN)
    for k in range(2):
        rows = near_ref[lines * k : lines * k + lines, :]
        total = total + mixed(rows, own_ref[128 * k : 128 * k + 128, :], NN)
    out_ref[...] = total * scale


def scores_of(near, far, own, other, scale):
    return pl.pallas_call(
        functools.partial(scores_kernel, scale),
        in_specs=[VMEM] * 4,
        out_specs=VMEM,
        out_shape=struct(near.shape[0] // 2, 128),
        cost_estimate=cost(1 << 29, 1 << 20),
        compiler_params=vmem(4),
        name="scores",
    )(near, far, own, other)


def to_each(lines, axis):
    count = lax.axis_size(axis)
    return lines.reshape(count, -1, lines.shape[-1])


def to_all(part, axis):
    return jnp.broadcast_to(part[None], (lax.axis_size(axis), *part.shape))


def exchanged(blocks, axis):
    return lax.all_to_all(blocks, axis, 0, 0, tiled=True)


def across(shard, bit):
    return lax.ppermute(shard, "cohort", [(i, i ^ bit) for i in range(lax.axis_size("cohort"))])


def after(value, *others):
    return lax.optimization_barrier((value, *others))[0]


def on_device(shapes, sketch_signs, merge_sketch):
    shapes, signs = shapes[0], sketch_signs[0]
    peers = lax.axis_size("coord")
    position = lax.axis_index("cohort")
    side = (position & 1).reshape(1)
    upper = (position >> 1 & 1).reshape(1)

    mean_given, own_given = sketched(1 - upper, shapes, signs)
    far_kept = across(own_given, 2)
    mean_kept, own_kept = sketched(upper, shapes, signs)
    mate_given = across(own_given, 1)
    mate_kept = across(own_kept, 1)
    pair = cross_grams((own_given, mate_given, own_given), (own_kept, mate_kept, own_kept))
    later = after(shapes, pair)
    pair = exchanged(to_each(pair, "coord"), "coord")
    near_sums = subject_sums(peers, 1 - upper, later, mean_given, own_given, mate_given)
    near_sums = subject_sums(peers, upper, later, mean_kept, own_kept, mate_kept, near_sums)
    pair_part = jnp.sum(pair, axis=0)
    lines = pair_part.shape[0]
    far_kept = after(far_kept, near_sums, pair_part)

    far_cross = cross_grams((own_kept, mate_kept, far_kept))
    far_given = across(after(own_kept, far_kept), 2)
    far_mate_kept = across(far_kept, 1)
    both = exchanged(
        jnp.concatenate([to_all(pair_part, "coord"), to_each(far_cross, "coord")], axis=1), "coord"
    )
    far_sums_kept = subject_sums(peers, upper, shapes, mean_kept, far_kept, far_mate_kept)
    near_sums = jnp.pad(near_sums, ((0, 0), (lines, 0), (0, 0)))
    both, near_sums, _ = lax.optimization_barrier((both, near_sums, far_sums_kept))
    far_part = jnp.sum(both[:, lines:], axis=0)
    far_cross = exchanged(
        lax.dynamic_update_slice(near_sums, to_all(far_part, "coord"), (0, 0, 0)), "coord"
    )

    own_map = own_level(side, both, merge_sketch)
    mate_map = across(own_map, 1)
    near = pair_level(own_map, mate_map, both, merge_sketch)
    far = across(near, 2)
    far_given = after(far_given, mate_map)
    far_mate_given = across(far_given, 1)
    far_sums = subject_sums(
        peers, 1 - upper, after(shapes, near), mean_given, far_given, far_mate_given
    )

    far_sums = far_terms(far_sums_kept, far_sums, far)
    far = after(far, far_sums)
    near_sums = jnp.sum(far_cross[:, lines:], axis=0)
    far_cross = far_cross_term(upper, near, far_cross, far)
    far_cross = far_cross + across(far_cross, 1)
    far_sums = exchanged(after(far_sums, far_cross), "coord")
    far_cross = far_cross + across(far_cross, 2)

    total = shapes.shape[1] * peers
    basis, own_map, other_map = last_level(
        upper,
        far_cross,
        merge_sketch,
        near,
        far,
        (own_kept, mate_kept, far_kept, far_mate_kept),
        (own_given, mate_given, far_given, far_mate_given),
        math.sqrt(total),
    )
    factor = 4.0 * math.sqrt(basis.shape[1] / total)
    scores = scores_of(near_sums, far_sums, own_map, other_map, factor)
    return basis[None], scores[None]


def solution(mesh):
    placed = (P("cohort", None, "coord"), P("cohort", None, None), P())
    return jax.shard_map(
        on_device,
        mesh=mesh,
        in_specs=placed,
        out_specs=(P("cohort", "coord", None), P("cohort", "coord", None)),
        check_vma=False,
    )
```
